32 devices in a mesh: groups: 2 (over y), feat: 4 (over z), rows: 2 (over x), sub: 2 (over core).
Axes of the slice: x: 2, y: 2, z: 4, core: 2. Of those that a mesh axis runs over, the one named last changes fastest.
Arguments:
- acts: bfloat16 [256, 32, 8192], P(('groups', 'rows', 'sub'), None, 'feat'), parts along dimension 0, may hold values from -6 to 6
- out_grads: bfloat16 [256, 32, 8192], P(('groups', 'rows', 'sub'), None, 'feat'), parts along dimension 0, may hold values from -6 to 6
- proj_in: bfloat16 [8192, 128], P('feat'), may hold values from -0.0625 to 0.0625
- proj_out: bfloat16 [8192, 128], P('feat'), may hold values from -0.0625 to 0.0625
- store: float32 [5120, 16384], P(('groups', 'rows', 'sub'), 'feat'), parts along dimension 0, may hold values from -0.0084 to 0.0084
Outputs:
- scores: float32 [256, 2560], P(('groups', 'feat'), ('rows', 'sub')), parts along dimension 0
The draws below stay inside these ranges and needn't reach their ends.
There are 2 independent parts, one for each index of `groups`. The reference program is written for one: setup_inputs(seed, part) draws one part's arguments, and reference() takes and returns one part's arrays. A program takes and returns all parts, laid end to end along the dimension named above; an argument that names none is the same for every part. Nothing has to cross between parts.
All inputs are finite; a program needn't handle non-finite values.
Results may differ from the reference program's by a relative error of at most 0.0003.
Values sent between devices are 32-bit elements; how exact they have to be, the bound alone decides.
No kernel may reach another device: no remote copies, remote signals or barrier semaphores. Data moves between devices by JAX's collectives and lax.ppermute only.
A program may use at most 64 MiB of HBM per device.

```python
import jax
import jax.numpy as jnp
from jax import lax

D = 8192
RANK = 128
TOK = 32
FEATS = 16384
QUERIES = 128
EXAMPLES = 2560


def steps_of(rng, extent, shards, least, largest):
    factor_of = 1.0
    for position, shards_of in shards:
        heights = jax.random.uniform(jax.random.fold_in(jax.random.fold_in(rng, 6), position), (shards_of,), jnp.float32, least / len(shards), largest / len(shards))
        factor_of = factor_of * jnp.repeat(jnp.exp(heights), extent[position] // shards_of).reshape((-1,) + (1,) * (len(extent) - 1 - position))
    return factor_of


def centred(rng, extent, spread, reach, cuts=(), kind=jnp.bfloat16):
    values = spread * jax.random.normal(rng, extent, jnp.float32)
    if cuts:
        values = values * steps_of(rng, extent, cuts, -0.22, 0.18)
    return jnp.clip(values, -reach, reach).astype(kind)


def setup_inputs(seed: int = 0, part: int = 0) -> dict:
    keys = jax.random.split(jax.random.key(seed), 6)
    part_splits = jax.random.split(jax.random.fold_in(keys[5], part), 6)
    acts = centred(part_splits[0], (QUERIES, TOK, D), 1.0, 6.0, ((0, 4), (2, 4)))
    out_grads = centred(part_splits[1], (QUERIES, TOK, D), 1.0, 6.0, ((0, 4), (2, 4)))
    proj_in = centred(keys[2], (D, RANK), D ** -0.5, 0.0625, ((0, 4),))
    proj_out = centred(keys[3], (D, RANK), D ** -0.5, 0.0625, ((0, 4),))
    store = centred(part_splits[4], (EXAMPLES, FEATS), 0.0014, 0.0084, ((0, 4), (1, 4)), jnp.float32)
    return {"acts": acts, "out_grads": out_grads, "proj_in": proj_in, "proj_out": proj_out, "store": store}


def reference(acts, out_grads, proj_in, proj_out, store):
    flat_acts = acts.reshape(QUERIES * TOK, D)
    flat_grads = out_grads.reshape(QUERIES * TOK, D)
    in_proj = jnp.dot(flat_acts, proj_in, preferred_element_type=jnp.float32).reshape(QUERIES, TOK, RANK)
    out_proj = jnp.dot(flat_grads, proj_out, preferred_element_type=jnp.float32).reshape(QUERIES, TOK, RANK)
    query_grad = jnp.einsum("qti,qtj->qij", out_proj.astype(jnp.float32), in_proj.astype(jnp.float32), precision=lax.Precision.HIGHEST).reshape(QUERIES, RANK * RANK)
    scores = lax.dot_general(query_grad, store, (((1,), (1,)), ((), ())), precision=lax.Precision.HIGHEST, preferred_element_type=jnp.float32)
    return scores
```

```python
import functools

import jax
import jax.numpy as jnp
from jax import lax
from jax.experimental import pallas as pl
from jax.experimental.pallas import tpu as pltpu
from jax.sharding import PartitionSpec as P

BF16, F32 = jnp.bfloat16, jnp.float32
NT = (((1,), (1,)), ((), ()))
NN = (((1,), (0,)), ((), ()))
VMEM_LIMIT = 48 * 1024 * 1024


def params(limit=VMEM_LIMIT):
    return pltpu.CompilerParams(vmem_limit_bytes=limit)


def whole(shape):
    return pl.BlockSpec(shape, lambda *_: (0,) * len(shape))


def in_vmem():
    return pl.BlockSpec(memory_space=pltpu.VMEM)


def gray(k):
    return k ^ (k >> 1)


def ungray(code):
    k = 0
    while code:
        k ^= code
        code >>= 1
    return k


def reversed_bits(value, bits):
    return sum(((value >> b) & 1) << (bits - 1 - b) for b in range(bits))


def exchange(x, axis, count, mask):
    return lax.ppermute(x, axis, [(k, k ^ mask) for k in range(count)])


def split(x):
    high = x.astype(BF16)
    return high, (x - high.astype(F32)).astype(BF16)


def in_kernel(tiles, x_ref, w_ref, keep_ref, send_ref):
    step = pl.program_id(0)
    rows = x_ref.shape[0]
    mine = gray(lax.axis_index("feat")) & 1
    half = tiles // 2
    product = jnp.dot(x_ref[...], w_ref[...], preferred_element_type=F32)
    place = pl.ds(pl.multiple_of(lax.rem(step, half) * rows, rows), rows)

    @pl.when(step // half == mine)
    def _():
        keep_ref[place, :] = product

    @pl.when(step // half != mine)
    def _():
        send_ref[place, :] = product


def project_in(x, w, tiles):
    rows, width = x.shape
    rank = w.shape[1]
    out = jax.ShapeDtypeStruct((rows // 2, rank), F32)
    return pl.pallas_call(
        functools.partial(in_kernel, tiles),
        grid=(tiles,),
        in_specs=[pl.BlockSpec((rows // tiles, width), lambda t: (t, 0)), whole(w.shape)],
        out_specs=[whole(out.shape)] * 2,
        out_shape=[out] * 2,
        compiler_params=params(),
        cost_estimate=pl.CostEstimate(
            flops=2 * rows * width * rank, bytes_accessed=2 * rows * width, transcendentals=0
        ),
        name="project_in",
    )(x, w)


def out_kernel(n, x_ref, w_ref, keep_ref, send_ref, turned):
    bits = n.bit_length() - 1
    here = lax.axis_index("feat")
    size = turned.shape[0] // n
    product = jnp.dot(x_ref[...], w_ref[...], preferred_element_type=F32)
    turned[...] = product.T
    for slot in range(n):
        chunk = here ^ ungray(reversed_bits(slot, bits))
        rows = turned[pl.ds(pl.multiple_of(chunk * size, size), size), :]
        ref = keep_ref if slot < n // 2 else send_ref
        ref[pl.ds(slot % (n // 2) * size, size), :] = rows


def project_out(x, w, tiles, n):
    rows, width = x.shape
    rank = w.shape[1]
    out = jax.ShapeDtypeStruct((rank // 2, rows), F32)
    columns = rows // tiles
    return pl.pallas_call(
        functools.partial(out_kernel, n),
        grid=(tiles,),
        in_specs=[pl.BlockSpec((columns, width), lambda t: (t, 0)), whole(w.shape)],
        out_specs=[pl.BlockSpec((rank // 2, columns), lambda t: (0, t))] * 2,
        out_shape=[out] * 2,
        scratch_shapes=[pltpu.VMEM((rank, columns), F32)],
        compiler_params=params(),
        cost_estimate=pl.CostEstimate(
            flops=2 * rows * width * rank, bytes_accessed=2 * rows * width, transcendentals=0
        ),
        name="project_out",
    )(x, w)


def outer_kernel(tokens, group, in_ref, out_ref, grad_ref):
    width = group * tokens
    features, rank = out_ref.shape[0], in_ref.shape[1]
    query = lax.broadcasted_iota(jnp.int32, (group, width), 0)
    token = lax.broadcasted_iota(jnp.int32, (group, width), 1)
    own = jnp.where(token // tokens == query, 1.0, 0.0).astype(F32)
    for g in range(in_ref.shape[0] // width):
        columns = out_ref[:, g * width : (g + 1) * width]
        spread = (columns[:, None, :] * own[None, :, :]).reshape(features * group, width)
        left, left_low = split(spread)
        right, right_low = split(in_ref[g * width : (g + 1) * width, :])
        total = jnp.dot(left, right, preferred_element_type=F32)
        total += jnp.dot(left_low, right, preferred_element_type=F32)
        total += jnp.dot(left, right_low, preferred_element_type=F32)
        grad_ref[:, g * group : (g + 1) * group, :] = total.reshape(features, group, rank)


def outer(in_rows, out_columns, tokens, group):
    rows, rank = in_rows.shape
    features = out_columns.shape[0]
    out = jax.ShapeDtypeStruct((features, rows // tokens, rank), F32)
    return pl.pallas_call(
        functools.partial(outer_kernel, tokens, group),
        in_specs=[in_vmem()] * 2,
        out_specs=in_vmem(),
        out_shape=out,
        compiler_params=params(),
        cost_estimate=pl.CostEstimate(
            flops=6 * rows * group * features * rank, bytes_accessed=8 * rows * rank, transcendentals=0
        ),
        name="outer",
    )(in_rows, out_columns)


def split_kernel(x_ref, high_ref, low_ref):
    high_ref[...], low_ref[...] = split(x_ref[...])


def split_store(store, tiles):
    rows, width = store.shape
    spec = pl.BlockSpec((rows // tiles, width), lambda t: (t, 0))
    out = jax.ShapeDtypeStruct(store.shape, BF16)
    return pl.pallas_call(
        split_kernel,
        grid=(tiles,),
        in_specs=[spec],
        out_specs=[spec] * 2,
        out_shape=[out] * 2,
        compiler_params=params(),
        cost_estimate=pl.CostEstimate(flops=rows * width, bytes_accessed=8 * rows * width, transcendentals=0),
        name="split_store",
    )(store)


def score_kernel(n, grads_ref, high_ref, low_ref, *rest):
    out_refs, (both,) = rest[:n], rest[n:]
    features, queries, rank = grads_ref.shape
    step = pl.program_id(0)
    here = lax.axis_index("feat")

    @pl.when(step == 0)
    def _():
        for i in range(features):
            high, low = split(grads_ref[i])
            both[:queries, i * rank : (i + 1) * rank] = high
            both[queries:, i * rank : (i + 1) * rank] = low

    total = lax.dot_general(high_ref[...], both[...], NT, preferred_element_type=F32)
    low = lax.dot_general(low_ref[...], both[:queries, :], NT, preferred_element_type=F32)
    total = total[:, :queries] + total[:, queries:] + low
    turned = total.T
    size = queries // n
    for slot in range(n):
        for k in range(n):
            @pl.when(here ^ slot == k)
            def _(slot=slot, k=k):
                out_refs[slot][...] = turned[k * size : (k + 1) * size, :]


def score(grads, high, low, n, tiles):
    features, queries, rank = grads.shape
    examples, width = high.shape
    spec = pl.BlockSpec((examples // tiles, width), lambda t: (t, 0))
    out = jax.ShapeDtypeStruct((queries // n, examples), F32)
    return pl.pallas_call(
        functools.partial(score_kernel, n),
        grid=(tiles,),
        in_specs=[whole(grads.shape), spec, spec],
        out_specs=[pl.BlockSpec((queries // n, examples // tiles), lambda t: (0, t))] * n,
        out_shape=[out] * n,
        scratch_shapes=[pltpu.VMEM((2 * queries, width), BF16)],
        compiler_params=params(),
        cost_estimate=pl.CostEstimate(
            flops=6 * queries * examples * width, bytes_accessed=4 * examples * width, transcendentals=0
        ),
        name="score",
    )(grads, high, low)


def tile_count(extent, unit, most):
    return next(t for t in range(most, 0, -1) if extent % (t * unit) == 0)


def local(sizes, acts, out_grads, proj_in, proj_out, store):
    n, rows, sub = sizes["feat"], sizes["rows"], sizes["sub"]
    bits = n.bit_length() - 1
    queries, tokens, width = acts.shape
    rank = proj_in.shape[1]
    here = gray(lax.axis_index("feat"))
    flat = queries * tokens

    in_keep, in_send = project_in(acts.reshape(flat, width), proj_in, 4)
    out_keep, out_send = project_out(out_grads.reshape(flat, width), proj_out, 4, n)

    in_sum = in_keep + exchange(in_send, "feat", n, 1)
    out_sum = out_keep + exchange(out_send, "feat", n, 1)
    for s in range(1, bits):
        mask = 2 ** (s + 1) - 1
        in_sum = in_sum + exchange(in_sum, "feat", n, mask)
        size = out_sum.shape[0] // 2
        out_sum = out_sum[:size] + exchange(out_sum[size:], "feat", n, mask)
    in_other = exchange(in_sum, "feat", n, 1)
    first = here & 1 == 0
    in_all = jnp.concatenate([jnp.where(first, in_sum, in_other), jnp.where(first, in_other, in_sum)])

    grads = outer(in_all, out_sum, tokens, 8)[None]
    for axis, count in (("rows", rows), ("sub", sub)):
        step = 1
        while step < count:
            other = exchange(grads, axis, count, step)
            low = lax.axis_index(axis) & step == 0
            grads = jnp.concatenate([jnp.where(low, grads, other), jnp.where(low, other, grads)])
            step *= 2
    features = grads.shape[1]
    grads = grads.reshape(sub, rows, features, queries, rank).transpose(2, 1, 0, 3, 4)
    grads = grads.reshape(features, rows * sub * queries, rank)
    high, low = split_store(store, tile_count(store.shape[0], 16, 5))
    parts = score(grads, high, low, n, tile_count(store.shape[0], 128, 5))
    total = parts[0]
    for mask in range(1, n):
        total = total + exchange(parts[mask], "feat", n, mask)
    return total


def solution(mesh):
    return jax.shard_map(
        functools.partial(local, dict(mesh.shape)),
        mesh=mesh,
        in_specs=(
            P(("groups", "rows", "sub"), None, "feat"),
            P(("groups", "rows", "sub"), None, "feat"),
            P("feat", None),
            P("feat", None),
            P(("groups", "rows", "sub"), "feat"),
        ),
        out_specs=P(("groups", "feat"), ("rows", "sub")),
        check_vma=False,
    )
```

```python
import functools

import jax
import jax.numpy as jnp
from jax import lax
from jax.experimental import pallas as pl
from jax.experimental.pallas import tpu as pltpu
from jax.sharding import PartitionSpec as P

BF16, F32 = jnp.bfloat16, jnp.float32
NT = (((1,), (1,)), ((), ()))
NN = (((1,), (0,)), ((), ()))
MIB = 1024 * 1024


def params(limit):
    return pltpu.CompilerParams(vmem_limit_bytes=limit * MIB)


def in_vmem():
    return pl.BlockSpec(memory_space=pltpu.VMEM)


def anywhere():
    return pl.BlockSpec(memory_space=pl.ANY)


def in_hbm():
    return pl.BlockSpec(memory_space=pltpu.HBM)


def gray(k):
    return k ^ (k >> 1)


def ungray(code):
    k = 0
    while code:
        k ^= code
        code >>= 1
    return k


def reversed_bits(value, bits):
    return sum(((value >> b) & 1) << (bits - 1 - b) for b in range(bits))


def exchange(x, axis, count, mask):
    return lax.ppermute(x, axis, [(k, k ^ mask) for k in range(count)])


def split(x):
    high = x.astype(BF16)
    return high, (x - high.astype(F32)).astype(BF16)


def in_kernel(tiles, x_ref, w_ref, out_ref, x_buf, w_buf, sems):
    rows = x_buf.shape[0]
    size = rows // tiles
    half = (gray(lax.axis_index("feat")) & 1) ^ 1
    w_copy = pltpu.make_async_copy(w_ref, w_buf, sems.at[tiles])
    w_copy.start()
    copies = []
    for t in range(tiles):
        place = pl.multiple_of(half * rows + t * size, size)
        copies.append(
            pltpu.make_async_copy(x_ref.at[pl.ds(place, size)], x_buf.at[pl.ds(t * size, size)], sems.at[t])
        )
        copies[t].start()
    w_copy.wait()
    for t in range(tiles):
        copies[t].wait()
        tile = slice(t * size, (t + 1) * size)
        out_ref[tile, :] = jnp.dot(x_buf[tile, :], w_buf[...], preferred_element_type=F32)


def project_sent(x, w, tiles):
    rows, width = x.shape
    rank = w.shape[1]
    return pl.pallas_call(
        functools.partial(in_kernel, tiles),
        in_specs=[in_hbm()] * 2,
        out_specs=in_vmem(),
        out_shape=jax.ShapeDtypeStruct((rows // 2, rank), F32),
        scratch_shapes=[
            pltpu.VMEM((rows // 2, width), BF16),
            pltpu.VMEM(w.shape, BF16),
            pltpu.SemaphoreType.DMA((tiles + 1,)),
        ],
        compiler_params=params(60),
        cost_estimate=pl.CostEstimate(flops=rows * width * rank, bytes_accessed=0, transcendentals=0),
        name="project_sent",
    )(x, w)


def rest_kernel(n, tiles, out_x_ref, out_w_ref, in_x_ref, in_w_ref, after_ref, keep_ref, send_ref, in_ref, *scratch):
    del after_ref
    out_buf, out_w, in_buf, in_w, turned, sems = scratch
    bits = n.bit_length() - 1
    here = lax.axis_index("feat")
    half = gray(here) & 1
    rows = in_buf.shape[0]
    size = rows // tiles
    copies = [(out_w_ref, out_w)]
    for t in range(2 * tiles):
        place = pl.ds(t * size, size)
        copies.append((out_x_ref.at[place], out_buf.at[place]))
    copies.append((in_w_ref, in_w))
    for t in range(tiles):
        place = pl.multiple_of(half * rows + t * size, size)
        copies.append((in_x_ref.at[pl.ds(place, size)], in_buf.at[pl.ds(t * size, size)]))
    copies = [pltpu.make_async_copy(*pair, sems.at[k]) for k, pair in enumerate(copies)]
    for copy in copies:
        copy.start()
    copies[0].wait()
    for t in range(2 * tiles):
        copies[1 + t].wait()
        tile = slice(t * size, (t + 1) * size)
        turned[:, tile] = jnp.dot(out_buf[tile, :], out_w[...], preferred_element_type=F32).T
    features = turned.shape[0] // n
    for slot in range(n):
        chunk = here ^ ungray(reversed_bits(slot, bits))
        ref = keep_ref if slot < n // 2 else send_ref
        place = slot % (n // 2) * features
        ref[place : place + features, :] = turned[pl.ds(pl.multiple_of(chunk * features, features), features), :]
    copies[1 + 2 * tiles].wait()
    for t in range(tiles):
        copies[2 + 2 * tiles + t].wait()
        tile = slice(t * size, (t + 1) * size)
        in_ref[tile, :] = jnp.dot(in_buf[tile, :], in_w[...], preferred_element_type=F32)


def project_rest(out_x, out_w, in_x, in_w, after, tiles, n):
    rows, width = out_x.shape
    rank = out_w.shape[1]
    out = jax.ShapeDtypeStruct((rank // 2, rows), F32)
    return pl.pallas_call(
        functools.partial(rest_kernel, n, tiles),
        in_specs=[in_hbm()] * 4 + [anywhere()],
        out_specs=[in_vmem()] * 3,
        out_shape=[out, out, jax.ShapeDtypeStruct((rows // 2, rank), F32)],
        scratch_shapes=[
            pltpu.VMEM((rows, width), BF16),
            pltpu.VMEM(out_w.shape, BF16),
            pltpu.VMEM((rows // 2, width), BF16),
            pltpu.VMEM(in_w.shape, BF16),
            pltpu.VMEM((rank, rows), F32),
            pltpu.SemaphoreType.DMA((3 * tiles + 2,)),
        ],
        compiler_params=params(57),
        cost_estimate=pl.CostEstimate(
            flops=3 * rows * width * rank, bytes_accessed=0, transcendentals=0
        ),
        name="project_rest",
    )(out_x, out_w, in_x, in_w, after)


def add_kernel(parts, a_ref, b_ref, *rest):
    out_refs = rest[len(rest) - parts :]
    size = a_ref.shape[0] // parts
    for k, out_ref in enumerate(out_refs):
        rows = slice(k * size, (k + 1) * size)
        out_ref[...] = a_ref[rows, :] + b_ref[rows, :]


def add(a, b, parts=1, after=(), weight=1):
    out = jax.ShapeDtypeStruct((a.shape[0] // parts, a.shape[1]), F32)
    return pl.pallas_call(
        functools.partial(add_kernel, parts),
        in_specs=[in_vmem()] * 2 + [anywhere()] * len(after),
        out_specs=[in_vmem()] * parts,
        out_shape=[out] * parts,
        compiler_params=params(8),
        cost_estimate=pl.CostEstimate(flops=weight * a.size, bytes_accessed=12 * a.size, transcendentals=0),
        name="add",
    )(a, b, *after)


def outer_kernel(tokens, group, second, in_ref, out_ref, *rest):
    grad_ref = rest[-1]
    width = group * tokens
    rows, rank = in_ref.shape
    features = out_ref.shape[0]
    half = (gray(lax.axis_index("feat")) & 1) ^ second
    query = lax.broadcasted_iota(jnp.int32, (group, width), 0)
    token = lax.broadcasted_iota(jnp.int32, (group, width), 1)
    own = jnp.where(token // tokens == query, 1.0, 0.0).astype(F32)
    for g in range(rows // width):
        columns = out_ref[:, pl.ds(pl.multiple_of(half * rows + g * width, width), width)]
        spread = (columns[:, None, :] * own[None, :, :]).reshape(features * group, width)
        left, left_low = split(spread)
        right, right_low = split(in_ref[g * width : (g + 1) * width, :])
        total = jnp.dot(left, right, preferred_element_type=F32)
        total += jnp.dot(left_low, right, preferred_element_type=F32)
        total += jnp.dot(left, right_low, preferred_element_type=F32)
        grad_ref[:, g * group : (g + 1) * group, :] = total.reshape(features, group, rank)


def outer(in_rows, out_columns, tokens, group, second, after=()):
    rows, rank = in_rows.shape
    features = out_columns.shape[0]
    out = jax.ShapeDtypeStruct((features, rows // tokens, rank), F32)
    return pl.pallas_call(
        functools.partial(outer_kernel, tokens, group, second),
        in_specs=[in_vmem()] * 2 + [anywhere()] * len(after),
        out_specs=in_vmem(),
        out_shape=out,
        compiler_params=params(16),
        cost_estimate=pl.CostEstimate(
            flops=6 * rows * group * features * rank, bytes_accessed=8 * rows * rank, transcendentals=0
        ),
        name="outer",
    )(in_rows, out_columns, *after)


def split_kernel(first, tiles, x_ref, after_ref, high_ref, low_ref, x_buf, sems):
    del after_ref
    size = x_buf.shape[0] // tiles
    copies = []
    for t in range(tiles):
        copies.append(
            pltpu.make_async_copy(x_ref.at[pl.ds(first + t * size, size)], x_buf.at[pl.ds(t * size, size)], sems.at[t])
        )
        copies[t].start()
    for t in range(tiles):
        copies[t].wait()
        rows = slice(t * size, (t + 1) * size)
        high_ref[rows, :], low_ref[rows, :] = split(x_buf[rows, :])


def split_store(store, after, start, rows):
    width = store.shape[1]
    tiles = tile_count(rows, 16, 5)
    out = jax.ShapeDtypeStruct((rows, width), BF16)
    return pl.pallas_call(
        functools.partial(split_kernel, start, tiles),
        in_specs=[in_hbm(), anywhere()],
        out_specs=[in_vmem()] * 2,
        out_shape=[out] * 2,
        scratch_shapes=[pltpu.VMEM((rows, width), F32), pltpu.SemaphoreType.DMA((tiles,))],
        compiler_params=params(24),
        cost_estimate=pl.CostEstimate(flops=1000 * rows * width, bytes_accessed=0, transcendentals=0),
        name="split_store",
    )(store, after)


def score_kernel(n, sub, count, *refs):
    store_refs, out_refs, (both, result) = refs[count : -n - 2], refs[-n - 2 : -2], refs[-2:]
    grad_refs = refs[:count]
    features, queries, rank = grad_refs[0].shape
    total = count * queries
    here = lax.axis_index("feat")
    half = gray(here) & 1
    for d in range(count // 2):
        for second in range(2):
            ref = grad_refs[2 * d + second]
            place = 2 * d * queries + (half ^ second) * queries
            place = pl.multiple_of(place, queries)
            for i in range(features):
                high, low = split(ref[i])
                both[pl.ds(place, queries), i * rank : (i + 1) * rank] = high
                both[pl.ds(total + place, queries), i * rank : (i + 1) * rank] = low
    first = 0
    for high_ref, low_ref in zip(store_refs[::2], store_refs[1::2]):
        sums = lax.dot_general(both[...], high_ref[...], NT, preferred_element_type=F32)
        lows = lax.dot_general(both[:total, :], low_ref[...], NT, preferred_element_type=F32)
        result[:, first : first + high_ref.shape[0]] = sums[:total] + sums[total:] + lows
        first += high_ref.shape[0]
    own = here ^ (lax.axis_index("rows") * sub + lax.axis_index("sub"))
    size = 2 * queries
    for slot in range(n):
        out_refs[slot][...] = result[pl.ds(pl.multiple_of((own ^ slot) * size, size), size), :]


def score(grads, stored, n, sub):
    features, queries, rank = grads[0].shape
    examples, width = sum(part.shape[0] for part in stored[::2]), stored[0].shape[1]
    total = len(grads) * queries
    out = jax.ShapeDtypeStruct((total // n, examples), F32)
    return pl.pallas_call(
        functools.partial(score_kernel, n, sub, len(grads)),
        in_specs=[in_vmem()] * (len(grads) + len(stored)),
        out_specs=[in_vmem()] * n,
        out_shape=[out] * n,
        scratch_shapes=[pltpu.VMEM((2 * total, width), BF16), pltpu.VMEM((total, examples), F32)],
        compiler_params=params(24),
        cost_estimate=pl.CostEstimate(
            flops=6 * total * examples * width, bytes_accessed=4 * examples * width, transcendentals=0
        ),
        name="score",
    )(*grads, *stored)


def tile_count(extent, unit, most):
    return next(t for t in range(most, 0, -1) if extent % (t * unit) == 0)


def gathered(own, sizes):
    arrays = [own]
    for axis in ("rows", "sub"):
        mask = 1
        while mask < sizes[axis]:
            arrays = arrays + [exchange(a, axis, sizes[axis], mask) for a in arrays]
            mask *= 2
    return arrays


def neighbours(sizes):
    order = [0]
    for axis, unit in (("rows", sizes["sub"]), ("sub", 1)):
        mask = 1
        while mask < sizes[axis]:
            order = order + [d ^ (mask * unit) for d in order]
            mask *= 2
    return order


def local(sizes, acts, out_grads, proj_in, proj_out, store):
    n, rows, sub = sizes["feat"], sizes["rows"], sizes["sub"]
    bits = n.bit_length() - 1
    queries, tokens, width = acts.shape
    flat = queries * tokens
    acts = acts.reshape(flat, width)
    out_grads = out_grads.reshape(flat, width)

    in_send = project_sent(acts, proj_in, 2)
    in_recv = exchange(in_send, "feat", n, 1)
    out_keep, out_send, in_keep = project_rest(out_grads, proj_out, acts, proj_in, in_send, 2, n)
    (in_sum,) = add(in_keep, in_recv)
    examples = store.shape[0]
    early = examples // 512 * 256
    stored = split_store(store, in_sum, 0, early) if early else []
    for s in range(1, bits):
        mask = 2 ** (s + 1) - 1
        in_recv = exchange(in_sum, "feat", n, mask)
        out_keep, out_send = add(out_keep, exchange(out_send, "feat", n, mask // 2), 2, stored[:1])
        out_recv = exchange(out_send, "feat", n, mask)
        (in_sum,) = add(in_sum, in_recv)
    stored = stored + split_store(store, in_sum, early, examples - early)
    (out_sum,) = add(out_keep, out_recv, 1, stored[-1:], weight=10**6)
    in_other = exchange(in_sum, "feat", n, 1)

    first = gathered(outer(in_sum, out_sum, tokens, 8, 0), sizes)
    second = gathered(outer(in_other, out_sum, tokens, 8, 1), sizes)
    order = neighbours(sizes)
    grads = [None] * (2 * len(order))
    for place, d in enumerate(order):
        grads[2 * d], grads[2 * d + 1] = first[place], second[place]
    parts = score(grads, stored, n, sub)
    moved = [exchange(parts[mask], "feat", n, mask) for mask in reversed(range(1, n))]
    total = parts[0]
    for part in reversed(moved):
        total = total + part
    return total


def solution(mesh):
    return jax.shard_map(
        functools.partial(local, dict(mesh.shape)),
        mesh=mesh,
        in_specs=(
            P(("groups", "rows", "sub"), None, "feat"),
            P(("groups", "rows", "sub"), None, "feat"),
            P("feat", None),
            P("feat", None),
            P(("groups", "rows", "sub"), "feat"),
        ),
        out_specs=P(("groups", "feat"), ("rows", "sub")),
        check_vma=False,
    )
```

```python
import functools

import jax
import jax.numpy as jnp
from jax import lax
from jax.experimental import pallas as pl
from jax.experimental.pallas import tpu as pltpu
from jax.sharding import PartitionSpec as P

BF16, F32 = jnp.bfloat16, jnp.float32
NT = (((1,), (1,)), ((), ()))
NN = (((1,), (0,)), ((), ()))
MIB = 1024 * 1024


def params(limit):
    return pltpu.CompilerParams(vmem_limit_bytes=limit * MIB)


def in_vmem():
    return pl.BlockSpec(memory_space=pltpu.VMEM)


def anywhere():
    return pl.BlockSpec(memory_space=pl.ANY)


def in_hbm():
    return pl.BlockSpec(memory_space=pltpu.HBM)


def gray(k):
    return k ^ (k >> 1)


def ungray(code):
    k = 0
    while code:
        k ^= code
        code >>= 1
    return k


def reversed_bits(value, bits):
    return sum(((value >> b) & 1) << (bits - 1 - b) for b in range(bits))


def exchange(x, axis, count, mask):
    return lax.ppermute(x, axis, [(k, k ^ mask) for k in range(count)])


def split(x):
    high = x.astype(BF16)
    return high, (x - high.astype(F32)).astype(BF16)


def sent_kernel(x_ref, w_ref, out_ref):
    rows = out_ref.shape[0]
    half = (gray(lax.axis_index("feat")) & 1) ^ 1
    place = pl.ds(pl.multiple_of(half * 2 * rows, rows), rows)
    out_ref[...] = jnp.dot(x_ref[place, :], w_ref[...], preferred_element_type=F32)


def project_sent(x, w):
    rows, width = x.shape
    rank = w.shape[1]
    return pl.pallas_call(
        sent_kernel,
        in_specs=[in_vmem()] * 2,
        out_specs=in_vmem(),
        out_shape=jax.ShapeDtypeStruct((rows // 4, rank), F32),
        compiler_params=params(16),
        cost_estimate=pl.CostEstimate(flops=rows * width * rank, bytes_accessed=rows * width, transcendentals=0),
        name="project_sent",
    )(x, w)


def rest_kernel(n, tiles, in_x_ref, in_w_ref, out_x_ref, out_w_ref, after_ref, *rest):
    del after_ref
    in_send_ref, in_first_ref, in_second_ref, out_keep_ref, out_send_ref, turned = rest
    bits = n.bit_length() - 1
    here = lax.axis_index("feat")
    half = gray(here) & 1
    rows = in_send_ref.shape[0]
    for ref, piece in (
        (in_send_ref, 2 * (half ^ 1) + 1),
        (in_first_ref, 2 * half),
        (in_second_ref, 2 * half + 1),
    ):
        place = pl.ds(pl.multiple_of(piece * rows, rows), rows)
        ref[...] = jnp.dot(in_x_ref[place, :], in_w_ref[...], preferred_element_type=F32)
    size = out_x_ref.shape[0] // tiles
    for t in range(tiles):
        tile = slice(t * size, (t + 1) * size)
        turned[:, tile] = jnp.dot(out_x_ref[tile, :], out_w_ref[...], preferred_element_type=F32).T
    features = turned.shape[0] // n
    for slot in range(n):
        chunk = here ^ ungray(reversed_bits(slot, bits))
        ref = out_keep_ref if slot < n // 2 else out_send_ref
        place = slot % (n // 2) * features
        ref[place : place + features, :] = turned[pl.ds(pl.multiple_of(chunk * features, features), features), :]


def project_rest(in_x, in_w, out_x, out_w, after, tiles, n):
    rows, width = out_x.shape
    rank = out_w.shape[1]
    piece = jax.ShapeDtypeStruct((rows // 4, rank), F32)
    out = jax.ShapeDtypeStruct((rank // 2, rows), F32)
    return pl.pallas_call(
        functools.partial(rest_kernel, n, tiles),
        in_specs=[in_vmem()] * 4 + [anywhere()],
        out_specs=[in_vmem()] * 5,
        out_shape=[piece] * 3 + [out] * 2,
        scratch_shapes=[pltpu.VMEM((rank, rows), F32)],
        compiler_params=params(16),
        cost_estimate=pl.CostEstimate(
            flops=3 * rows * width * rank, bytes_accessed=3 * rows * width, transcendentals=0
        ),
        name="project_rest",
    )(in_x, in_w, out_x, out_w, after)


def add_kernel(parts, a_ref, b_ref, *rest):
    out_refs = rest[len(rest) - parts :]
    size = a_ref.shape[0] // parts
    for k, out_ref in enumerate(out_refs):
        rows = slice(k * size, (k + 1) * size)
        out_ref[...] = a_ref[rows, :] + b_ref[rows, :]


def add(a, b, parts=1, after=(), weight=0.1):
    out = jax.ShapeDtypeStruct((a.shape[0] // parts, a.shape[1]), F32)
    return pl.pallas_call(
        functools.partial(add_kernel, parts),
        in_specs=[in_vmem()] * 2 + [anywhere()] * len(after),
        out_specs=[in_vmem()] * parts,
        out_shape=[out] * parts,
        compiler_params=params(8),
        cost_estimate=pl.CostEstimate(flops=int(weight * 1e9), bytes_accessed=12 * a.size, transcendentals=0),
        name="add",
    )(a, b, *after)


def add_beside_kernel(a_ref, b_ref, other_ref, sum_ref, same_ref):
    sum_ref[...] = a_ref[...] + b_ref[...]
    same_ref[...] = other_ref[...]


def add_beside(a, b, other, weight):
    return pl.pallas_call(
        add_beside_kernel,
        in_specs=[in_vmem()] * 3,
        out_specs=[in_vmem()] * 2,
        out_shape=[jax.ShapeDtypeStruct(a.shape, F32), jax.ShapeDtypeStruct(other.shape, F32)],
        compiler_params=params(8),
        cost_estimate=pl.CostEstimate(flops=int(weight * 1e9), bytes_accessed=12 * a.size, transcendentals=0),
        name="add_beside",
    )(a, b, other)


def outer_kernel(tokens, group, *refs):
    in_refs, (out_ref, grad_ref) = refs[:-2], refs[-2:]
    width = group * tokens
    rows, rank = in_refs[0].shape
    features = out_ref.shape[0]
    mine = gray(lax.axis_index("feat")) & 1
    query = lax.broadcasted_iota(jnp.int32, (group, width), 0)
    token = lax.broadcasted_iota(jnp.int32, (group, width), 1)
    own = jnp.where(token // tokens == query, 1.0, 0.0).astype(F32)
    for k, in_ref in enumerate(in_refs):
        half = mine ^ (k // 2)
        for g in range(rows // width):
            step = half * (2 * rows // width) + (k % 2) * (rows // width) + g
            columns = out_ref[:, pl.ds(pl.multiple_of(step * width, width), width)]
            spread = (columns[:, None, :] * own[None, :, :]).reshape(features * group, width)
            left, left_low = split(spread)
            right, right_low = split(in_ref[g * width : (g + 1) * width, :])
            total = jnp.dot(left, right, preferred_element_type=F32)
            total += jnp.dot(left_low, right, preferred_element_type=F32)
            total += jnp.dot(left, right_low, preferred_element_type=F32)
            place = pl.ds(pl.multiple_of(step * group, group), group)
            grad_ref[:, place, :] = total.reshape(features, group, rank)


def outer(in_pieces, out_columns, tokens, group):
    rank = in_pieces[0].shape[1]
    features, rows = out_columns.shape
    out = jax.ShapeDtypeStruct((features, rows // tokens, rank), F32)
    return pl.pallas_call(
        functools.partial(outer_kernel, tokens, group),
        in_specs=[in_vmem()] * (len(in_pieces) + 1),
        out_specs=in_vmem(),
        out_shape=out,
        compiler_params=params(16),
        cost_estimate=pl.CostEstimate(
            flops=6 * rows * group * features * rank, bytes_accessed=8 * rows * rank, transcendentals=0
        ),
        name="outer",
    )(*in_pieces, out_columns)


def split_kernel(first, tiles, x_ref, after_ref, high_ref, low_ref, x_buf, sems):
    del after_ref
    size = x_buf.shape[0] // tiles
    copies = []
    for t in range(tiles):
        copies.append(
            pltpu.make_async_copy(x_ref.at[pl.ds(first + t * size, size)], x_buf.at[pl.ds(t * size, size)], sems.at[t])
        )
        copies[t].start()
    for t in range(tiles):
        copies[t].wait()
        rows = slice(t * size, (t + 1) * size)
        high_ref[rows, :], low_ref[rows, :] = split(x_buf[rows, :])


def split_store(store, after, start, rows):
    width = store.shape[1]
    tiles = tile_count(rows, 16, 5)
    out = jax.ShapeDtypeStruct((rows, width), BF16)
    return pl.pallas_call(
        functools.partial(split_kernel, start, tiles),
        in_specs=[in_hbm(), anywhere()],
        out_specs=[in_vmem()] * 2,
        out_shape=[out] * 2,
        scratch_shapes=[pltpu.VMEM((rows, width), F32), pltpu.SemaphoreType.DMA((tiles,))],
        compiler_params=params(24),
        cost_estimate=pl.CostEstimate(flops=1000 * rows * width, bytes_accessed=0, transcendentals=0),
        name="split_store",
    )(store, after)


def score_kernel(n, sub, count, *refs):
    store_refs, out_refs, (both, result) = refs[count : -n - 2], refs[-n - 2 : -2], refs[-2:]
    grad_refs = refs[:count]
    features, queries, rank = grad_refs[0].shape
    total = count * queries
    for d, ref in enumerate(grad_refs):
        place = d * queries
        for i in range(features):
            high, low = split(ref[i])
            both[place : place + queries, i * rank : (i + 1) * rank] = high
            both[total + place : total + place + queries, i * rank : (i + 1) * rank] = low
    first = 0
    for high_ref, low_ref in zip(store_refs[::2], store_refs[1::2]):
        sums = lax.dot_general(both[...], high_ref[...], NT, preferred_element_type=F32)
        lows = lax.dot_general(both[:total, :], low_ref[...], NT, preferred_element_type=F32)
        result[:, first : first + high_ref.shape[0]] = sums[:total] + sums[total:] + lows
        first += high_ref.shape[0]
    own = lax.axis_index("feat") ^ (lax.axis_index("rows") * sub + lax.axis_index("sub"))
    size = queries
    for slot in range(n):
        out_refs[slot][...] = result[pl.ds(pl.multiple_of((own ^ slot) * size, size), size), :]


def score(grads, stored, n, sub):
    features, queries, rank = grads[0].shape
    examples, width = sum(part.shape[0] for part in stored[::2]), stored[0].shape[1]
    total = len(grads) * queries
    out = jax.ShapeDtypeStruct((total // n, examples), F32)
    return pl.pallas_call(
        functools.partial(score_kernel, n, sub, len(grads)),
        in_specs=[in_vmem()] * (len(grads) + len(stored)),
        out_specs=[in_vmem()] * n,
        out_shape=[out] * n,
        scratch_shapes=[pltpu.VMEM((2 * total, width), BF16), pltpu.VMEM((total, examples), F32)],
        compiler_params=params(24),
        cost_estimate=pl.CostEstimate(
            flops=6 * total * examples * width, bytes_accessed=4 * examples * width, transcendentals=0
        ),
        name="score",
    )(*grads, *stored)


def tile_count(extent, unit, most):
    return next(t for t in range(most, 0, -1) if extent % (t * unit) == 0)


def local(sizes, acts, out_grads, proj_in, proj_out, store):
    n, rows, sub = sizes["feat"], sizes["rows"], sizes["sub"]
    bits = n.bit_length() - 1
    queries, tokens, width = acts.shape
    flat = queries * tokens
    acts = acts.reshape(flat, width)
    out_grads = out_grads.reshape(flat, width)

    in_send = project_sent(acts, proj_in)
    in_recv = exchange(in_send, "feat", n, 1)
    in_send, *in_keep, out_keep, out_send = project_rest(acts, proj_in, out_grads, proj_out, in_send, 4, n)
    piece, out_send = add_beside(in_keep[0], in_recv, out_send, 2)
    pieces = [piece, *add(in_keep[1], exchange(in_send, "feat", n, 1), 1, (piece,), 1)]
    examples = store.shape[0]
    early = examples // 512 * 256
    stored = split_store(store, pieces[1], 0, early) if early else []
    for s in range(1, bits):
        mask = 2 ** (s + 1) - 1
        in_recvs = [exchange(piece, "feat", n, mask) for piece in pieces]
        out_keep, out_send = add(out_keep, exchange(out_send, "feat", n, mask // 2), 2, stored[:1])
        out_recv = exchange(out_send, "feat", n, mask)
        (first,) = add(pieces[0], in_recvs[0], 1, (), 1)
        pieces = [first, *add(pieces[1], in_recvs[1], 1, (first,), 1)]
    stored = stored + split_store(store, pieces[1], early, examples - early)
    (out_sum,) = add(out_keep, out_recv, 1, stored[-1:], weight=20)
    others = [exchange(piece, "feat", n, 1) for piece in pieces]

    blocks = [(0, [*pieces, *others], out_sum)]
    mask = 1
    while mask < rows:
        for d, block, out in list(blocks):
            parts = [exchange(part, "rows", rows, mask) for part in (*block, out)]
            blocks.append((d ^ (mask * sub), parts[:-1], parts[-1]))
        mask *= 2
    grads = {d: outer(block, out, tokens, 8) for d, block, out in blocks}
    mask = 1
    while mask < sub:
        for d, grad in list(grads.items()):
            grads[d ^ mask] = exchange(grad, "sub", sub, mask)
        mask *= 2
    grads = [grads[d] for d in range(len(grads))]
    parts = score(grads, stored, n, sub)
    moved = [exchange(parts[mask], "feat", n, mask) for mask in reversed(range(1, n))]
    total = parts[0]
    for part in reversed(moved):
        total = total + part
    return total


def solution(mesh):
    return jax.shard_map(
        functools.partial(local, dict(mesh.shape)),
        mesh=mesh,
        in_specs=(
            P(("groups", "rows", "sub"), None, "feat"),
            P(("groups", "rows", "sub"), None, "feat"),
            P("feat", None),
            P("feat", None),
            P(("groups", "rows", "sub"), "feat"),
        ),
        out_specs=P(("groups", "feat"), ("rows", "sub")),
        check_vma=False,
    )
```

```python
import functools

import jax
import jax.numpy as jnp
from jax import lax
from jax.experimental import pallas as pl
from jax.experimental.pallas import tpu as pltpu
from jax.sharding import PartitionSpec as P

BF16, F32 = jnp.bfloat16, jnp.float32
NT = (((1,), (1,)), ((), ()))
NN = (((1,), (0,)), ((), ()))
MIB = 1024 * 1024


def params(limit):
    return pltpu.CompilerParams(vmem_limit_bytes=limit * MIB)


def in_vmem():
    return pl.BlockSpec(memory_space=pltpu.VMEM)


def anywhere():
    return pl.BlockSpec(memory_space=pl.ANY)


def in_hbm():
    return pl.BlockSpec(memory_space=pltpu.HBM)


def gray(k):
    return k ^ (k >> 1)


def ungray(code):
    k = 0
    while code:
        k ^= code
        code >>= 1
    return k


def reversed_bits(value, bits):
    return sum(((value >> b) & 1) << (bits - 1 - b) for b in range(bits))


def exchange(x, axis, count, mask):
    return lax.ppermute(x, axis, [(k, k ^ mask) for k in range(count)])


def split(x):
    high = x.astype(BF16)
    return high, (x - high.astype(F32)).astype(BF16)


def sent_kernel(x_ref, w_ref, out_ref):
    rows = out_ref.shape[0]
    half = (gray(lax.axis_index("feat")) & 1) ^ 1
    place = pl.ds(pl.multiple_of(half * 2 * rows, rows), rows)
    out_ref[...] = jnp.dot(x_ref[place, :], w_ref[...], preferred_element_type=F32)


def project_sent(x, w):
    rows, width = x.shape
    rank = w.shape[1]
    return pl.pallas_call(
        sent_kernel,
        in_specs=[in_vmem()] * 2,
        out_specs=in_vmem(),
        out_shape=jax.ShapeDtypeStruct((rows // 4, rank), F32),
        compiler_params=params(16),
        cost_estimate=pl.CostEstimate(flops=rows * width * rank, bytes_accessed=rows * width, transcendentals=0),
        name="project_sent",
    )(x, w)


def rest_kernel(x_ref, w_ref, after_ref, send_ref, first_ref, second_ref):
    del after_ref
    half = gray(lax.axis_index("feat")) & 1
    rows = send_ref.shape[0]
    for ref, piece in ((send_ref, 2 * (half ^ 1) + 1), (first_ref, 2 * half), (second_ref, 2 * half + 1)):
        place = pl.ds(pl.multiple_of(piece * rows, rows), rows)
        ref[...] = jnp.dot(x_ref[place, :], w_ref[...], preferred_element_type=F32)


def project_rest(x, w, after):
    rows, width = x.shape
    rank = w.shape[1]
    return pl.pallas_call(
        rest_kernel,
        in_specs=[in_vmem()] * 2 + [anywhere()],
        out_specs=[in_vmem()] * 3,
        out_shape=[jax.ShapeDtypeStruct((rows // 4, rank), F32)] * 3,
        compiler_params=params(16),
        cost_estimate=pl.CostEstimate(flops=rows * width * rank, bytes_accessed=rows * width, transcendentals=0),
        name="project_rest",
    )(x, w, after)


def out_kernel(n, tiles, x_ref, w_ref, after_ref, keep_ref, send_ref, turned):
    del after_ref
    bits = n.bit_length() - 1
    here = lax.axis_index("feat")
    size = x_ref.shape[0] // tiles
    for t in range(tiles):
        tile = slice(t * size, (t + 1) * size)
        turned[:, tile] = jnp.dot(x_ref[tile, :], w_ref[...], preferred_element_type=F32).T
    features = turned.shape[0] // n
    for slot in range(n):
        chunk = here ^ ungray(reversed_bits(slot, bits))
        ref = keep_ref if slot < n // 2 else send_ref
        place = slot % (n // 2) * features
        ref[place : place + features, :] = turned[pl.ds(pl.multiple_of(chunk * features, features), features), :]


def project_out(x, w, after, tiles, n):
    rows, width = x.shape
    rank = w.shape[1]
    out = jax.ShapeDtypeStruct((rank // 2, rows), F32)
    return pl.pallas_call(
        functools.partial(out_kernel, n, tiles),
        in_specs=[in_vmem()] * 2 + [anywhere()],
        out_specs=[in_vmem()] * 2,
        out_shape=[out] * 2,
        scratch_shapes=[pltpu.VMEM((rank, rows), F32)],
        compiler_params=params(16),
        cost_estimate=pl.CostEstimate(
            flops=int(0.5 * 1e9), bytes_accessed=2 * rows * width, transcendentals=0
        ),
        name="project_out",
    )(x, w, after)


def add_kernel(parts, a_ref, b_ref, *rest):
    out_refs = rest[len(rest) - parts :]
    size = a_ref.shape[0] // parts
    for k, out_ref in enumerate(out_refs):
        rows = slice(k * size, (k + 1) * size)
        out_ref[...] = a_ref[rows, :] + b_ref[rows, :]


def add(a, b, parts=1, after=(), weight=0.1):
    out = jax.ShapeDtypeStruct((a.shape[0] // parts, a.shape[1]), F32)
    return pl.pallas_call(
        functools.partial(add_kernel, parts),
        in_specs=[in_vmem()] * 2 + [anywhere()] * len(after),
        out_specs=[in_vmem()] * parts,
        out_shape=[out] * parts,
        compiler_params=params(8),
        cost_estimate=pl.CostEstimate(flops=int(weight * 1e9), bytes_accessed=12 * a.size, transcendentals=0),
        name="add",
    )(a, b, *after)


def add_beside_kernel(a_ref, b_ref, other_ref, sum_ref, same_ref):
    sum_ref[...] = a_ref[...] + b_ref[...]
    same_ref[...] = other_ref[...]


def add_beside(a, b, other, weight):
    return pl.pallas_call(
        add_beside_kernel,
        in_specs=[in_vmem()] * 3,
        out_specs=[in_vmem()] * 2,
        out_shape=[jax.ShapeDtypeStruct(a.shape, F32), jax.ShapeDtypeStruct(other.shape, F32)],
        compiler_params=params(8),
        cost_estimate=pl.CostEstimate(flops=int(weight * 1e9), bytes_accessed=12 * a.size, transcendentals=0),
        name="add_beside",
    )(a, b, other)


def outer_kernel(tokens, group, part, *refs):
    in_refs, (out_ref, grad_ref) = refs[:4], (refs[4], refs[-1])
    width = group * tokens
    rows, rank = in_refs[0].shape
    features = grad_ref.shape[0]
    mine = gray(lax.axis_index("feat")) & 1
    query = lax.broadcasted_iota(jnp.int32, (group, width), 0)
    token = lax.broadcasted_iota(jnp.int32, (group, width), 1)
    own = jnp.where(token // tokens == query, 1.0, 0.0).astype(F32)
    for k, in_ref in enumerate(in_refs):
        half = mine ^ (k // 2)
        for g in range(rows // width):
            step = half * (2 * rows // width) + (k % 2) * (rows // width) + g
            lines = slice(part * features, (part + 1) * features)
            columns = out_ref[lines, pl.ds(pl.multiple_of(step * width, width), width)]
            spread = (columns[:, None, :] * own[None, :, :]).reshape(features * group, width)
            left, left_low = split(spread)
            right, right_low = split(in_ref[g * width : (g + 1) * width, :])
            total = jnp.dot(left, right, preferred_element_type=F32)
            total += jnp.dot(left_low, right, preferred_element_type=F32)
            total += jnp.dot(left, right_low, preferred_element_type=F32)
            place = pl.ds(pl.multiple_of(step * group, group), group)
            grad_ref[:, place, :] = total.reshape(features, group, rank)


def outer(in_pieces, out_columns, tokens, group, part, parts, after=()):
    rank = in_pieces[0].shape[1]
    features, rows = out_columns.shape[0] // parts, out_columns.shape[1]
    out = jax.ShapeDtypeStruct((features, rows // tokens, rank), F32)
    return pl.pallas_call(
        functools.partial(outer_kernel, tokens, group, part),
        in_specs=[in_vmem()] * (len(in_pieces) + 1) + [anywhere()] * len(after),
        out_specs=in_vmem(),
        out_shape=out,
        compiler_params=params(16),
        cost_estimate=pl.CostEstimate(
            flops=6 * rows * group * features * rank, bytes_accessed=8 * rows * rank, transcendentals=0
        ),
        name="outer",
    )(*in_pieces, out_columns, *after)


def split_kernel(first, tiles, x_ref, after_ref, high_ref, low_ref, x_buf, sems):
    del after_ref
    size = x_buf.shape[0] // tiles
    copies = []
    for t in range(tiles):
        copies.append(
            pltpu.make_async_copy(x_ref.at[pl.ds(first + t * size, size)], x_buf.at[pl.ds(t * size, size)], sems.at[t])
        )
        copies[t].start()
    for t in range(tiles):
        copies[t].wait()
        rows = slice(t * size, (t + 1) * size)
        high_ref[rows, :], low_ref[rows, :] = split(x_buf[rows, :])


def split_store(store, after, start, rows):
    width = store.shape[1]
    tiles = tile_count(rows, 16, 5)
    out = jax.ShapeDtypeStruct((rows, width), BF16)
    return pl.pallas_call(
        functools.partial(split_kernel, start, tiles),
        in_specs=[in_hbm(), anywhere()],
        out_specs=[in_vmem()] * 2,
        out_shape=[out] * 2,
        scratch_shapes=[pltpu.VMEM((rows, width), F32), pltpu.SemaphoreType.DMA((tiles,))],
        compiler_params=params(24),
        cost_estimate=pl.CostEstimate(flops=1000 * rows * width, bytes_accessed=0, transcendentals=0),
        name="split_store",
    )(store, after)


def products(grad_refs, store_refs, both, part):
    features, queries, rank = grad_refs[0].shape
    total = len(grad_refs) * queries
    for d, ref in enumerate(grad_refs):
        place = d * queries
        for i in range(features):
            high, low = split(ref[i])
            both[place : place + queries, i * rank : (i + 1) * rank] = high
            both[total + place : total + place + queries, i * rank : (i + 1) * rank] = low
    columns = slice(part * features * rank, (part + 1) * features * rank)
    first = 0
    for high_ref, low_ref in zip(store_refs[::2], store_refs[1::2]):
        sums = lax.dot_general(both[...], high_ref[:, columns], NT, preferred_element_type=F32)
        lows = lax.dot_general(both[:total, :], low_ref[:, columns], NT, preferred_element_type=F32)
        yield slice(first, first + high_ref.shape[0]), sums[:total] + sums[total:] + lows
        first += high_ref.shape[0]


def early_kernel(count, part, *refs):
    store_refs, (result_ref, both) = refs[count:-2], refs[-2:]
    for place, value in products(refs[:count], store_refs, both, part):
        result_ref[:, place] = value


def score_kernel(n, sub, count, part, *refs):
    early_refs, refs = refs[:part], refs[part:]
    store_refs, out_refs, (both, result) = refs[count : -n - 2], refs[-n - 2 : -2], refs[-2:]
    queries = refs[0].shape[1]
    for place, value in products(refs[:count], store_refs, both, part):
        for early_ref in early_refs:
            value = value + early_ref[:, place]
        result[:, place] = value
    own = lax.axis_index("feat") ^ (lax.axis_index("rows") * sub + lax.axis_index("sub"))
    for slot in range(n):
        out_refs[slot][...] = result[pl.ds(pl.multiple_of((own ^ slot) * queries, queries), queries), :]


def score(grads, stored, n, sub, part, parts, early):
    features, queries, rank = grads[0].shape
    examples, width = sum(block.shape[0] for block in stored[::2]), features * rank
    total = len(grads) * queries
    last = part == parts - 1
    if last:
        kernel = functools.partial(score_kernel, n, sub, len(grads), part)
        outs = [jax.ShapeDtypeStruct((total // n, examples), F32)] * n
        scratch = [pltpu.VMEM((total, examples), F32)]
    else:
        kernel = functools.partial(early_kernel, len(grads), part)
        outs, scratch = [jax.ShapeDtypeStruct((total, examples), F32)], []
        early = []
    return pl.pallas_call(
        kernel,
        in_specs=[in_vmem()] * (len(early) + len(grads) + len(stored)),
        out_specs=[in_vmem()] * len(outs),
        out_shape=outs,
        scratch_shapes=[pltpu.VMEM((2 * total, width), BF16), *scratch],
        compiler_params=params(24),
        cost_estimate=pl.CostEstimate(
            flops=6 * total * examples * width, bytes_accessed=4 * examples * width, transcendentals=0
        ),
        name="score",
    )(*early, *grads, *stored)


def tile_count(extent, unit, most):
    return next(t for t in range(most, 0, -1) if extent % (t * unit) == 0)


def local(sizes, acts, out_grads, proj_in, proj_out, store):
    n, rows, sub = sizes["feat"], sizes["rows"], sizes["sub"]
    bits = n.bit_length() - 1
    queries, tokens, width = acts.shape
    flat = queries * tokens
    acts = acts.reshape(flat, width)
    out_grads = out_grads.reshape(flat, width)

    in_send = project_sent(acts, proj_in)
    in_recv = exchange(in_send, "feat", n, 1)
    in_send, *in_keep = project_rest(acts, proj_in, in_send)
    out_keep, out_send = project_out(out_grads, proj_out, in_send, 4, n)
    piece, out_send = add_beside(in_keep[0], in_recv, out_send, 2)
    pieces = [piece, *add(in_keep[1], exchange(in_send, "feat", n, 1), 1, (piece,), 1)]
    examples = store.shape[0]
    early = examples // 512 * 256
    stored = split_store(store, pieces[1], 0, early) if early else []
    for s in range(1, bits):
        mask = 2 ** (s + 1) - 1
        in_recvs = [exchange(piece, "feat", n, mask) for piece in pieces]
        out_keep, out_send = add(out_keep, exchange(out_send, "feat", n, mask // 2), 2, stored[:1])
        out_recv = exchange(out_send, "feat", n, mask)
        (first,) = add(pieces[0], in_recvs[0], 1, (), 1)
        pieces = [first, *add(pieces[1], in_recvs[1], 1, (first,), 1)]
    stored = stored + split_store(store, pieces[1], early, examples - early)
    (out_sum,) = add(out_keep, out_recv, 1, stored[-1:], weight=20)
    others = [exchange(piece, "feat", n, 1) for piece in pieces]

    blocks = [(0, [*pieces, *others], out_sum)]
    mask = 1
    while mask < rows:
        for d, block, out in list(blocks):
            parts = [exchange(part, "rows", rows, mask) for part in (*block, out)]
            blocks.append((d ^ (mask * sub), parts[:-1], parts[-1]))
        mask *= 2
    parts = 2 if out_sum.shape[0] % 16 == 0 else 1
    grads = [{} for _ in range(parts)]
    after = ()
    for d, block, out in blocks:
        for part in range(parts):
            grads[part][d] = outer(block, out, tokens, 8, part, parts, after)
        after = (grads[-1][d],)
    early = []
    for part in range(parts):
        mask = 1
        while mask < sub:
            for d, grad in list(grads[part].items()):
                grads[part][d ^ mask] = exchange(grad, "sub", sub, mask)
            mask *= 2
        ordered = [grads[part][d] for d in range(len(grads[part]))]
        scores = score(ordered, stored, n, sub, part, parts, early)
        early = early + list(scores)
    total = scores[0]
    for mask in reversed(range(1, n)):
        (total,) = add(total, exchange(scores[mask], "feat", n, mask), 1, (), 1)
    return total


def solution(mesh):
    return jax.shard_map(
        functools.partial(local, dict(mesh.shape)),
        mesh=mesh,
        in_specs=(
            P(("groups", "rows", "sub"), None, "feat"),
            P(("groups", "rows", "sub"), None, "feat"),
            P("feat", None),
            P("feat", None),
            P(("groups", "rows", "sub"), "feat"),
        ),
        out_specs=P(("groups", "feat"), ("rows", "sub")),
        check_vma=False,
    )
```

```python
import functools

import jax
import jax.numpy as jnp
from jax import lax
from jax.experimental import pallas as pl
from jax.experimental.pallas import tpu as pltpu
from jax.sharding import PartitionSpec as P

BF16, F32 = jnp.bfloat16, jnp.float32
NT = (((1,), (1,)), ((), ()))
NN = (((1,), (0,)), ((), ()))
MIB = 1024 * 1024


def params(limit):
    return pltpu.CompilerParams(vmem_limit_bytes=limit * MIB)


def in_vmem():
    return pl.BlockSpec(memory_space=pltpu.VMEM)


def anywhere():
    return pl.BlockSpec(memory_space=pl.ANY)


def in_hbm():
    return pl.BlockSpec(memory_space=pltpu.HBM)


def gray(k):
    return k ^ (k >> 1)


def ungray(code):
    k = 0
    while code:
        k ^= code
        code >>= 1
    return k


def reversed_bits(value, bits):
    return sum(((value >> b) & 1) << (bits - 1 - b) for b in range(bits))


def exchange(x, axis, count, mask):
    return lax.ppermute(x, axis, [(k, k ^ mask) for k in range(count)])


def split(x):
    high = x.astype(BF16)
    return high, (x - high.astype(F32)).astype(BF16)


def sent_kernel(x_ref, w_ref, out_ref):
    rows = out_ref.shape[0]
    half = (gray(lax.axis_index("feat")) & 1) ^ 1
    place = pl.ds(pl.multiple_of(half * 2 * rows, rows), rows)
    out_ref[...] = jnp.dot(x_ref[place, :], w_ref[...], preferred_element_type=F32)


def project_sent(x, w):
    rows, width = x.shape
    rank = w.shape[1]
    return pl.pallas_call(
        sent_kernel,
        in_specs=[in_vmem()] * 2,
        out_specs=in_vmem(),
        out_shape=jax.ShapeDtypeStruct((rows // 4, rank), F32),
        compiler_params=params(16),
        cost_estimate=pl.CostEstimate(flops=rows * width * rank, bytes_accessed=rows * width, transcendentals=0),
        name="project_sent",
    )(x, w)


def rest_kernel(x_ref, w_ref, after_ref, send_ref, first_ref, second_ref):
    del after_ref
    half = gray(lax.axis_index("feat")) & 1
    rows = send_ref.shape[0]
    for ref, piece in ((send_ref, 2 * (half ^ 1) + 1), (first_ref, 2 * half), (second_ref, 2 * half + 1)):
        place = pl.ds(pl.multiple_of(piece * rows, rows), rows)
        ref[...] = jnp.dot(x_ref[place, :], w_ref[...], preferred_element_type=F32)


def project_rest(x, w, after):
    rows, width = x.shape
    rank = w.shape[1]
    return pl.pallas_call(
        rest_kernel,
        in_specs=[in_vmem()] * 2 + [anywhere()],
        out_specs=[in_vmem()] * 3,
        out_shape=[jax.ShapeDtypeStruct((rows // 4, rank), F32)] * 3,
        compiler_params=params(16),
        cost_estimate=pl.CostEstimate(flops=rows * width * rank, bytes_accessed=rows * width, transcendentals=0),
        name="project_rest",
    )(x, w, after)


def out_kernel(n, tiles, x_ref, w_ref, after_ref, keep_ref, send_ref, turned):
    del after_ref
    bits = n.bit_length() - 1
    here = lax.axis_index("feat")
    size = x_ref.shape[0] // tiles
    for t in range(tiles):
        tile = slice(t * size, (t + 1) * size)
        turned[:, tile] = jnp.dot(x_ref[tile, :], w_ref[...], preferred_element_type=F32).T
    features = turned.shape[0] // n
    for slot in range(n):
        chunk = here ^ ungray(reversed_bits(slot, bits))
        ref = keep_ref if slot < n // 2 else send_ref
        place = slot % (n // 2) * features
        ref[place : place + features, :] = turned[pl.ds(pl.multiple_of(chunk * features, features), features), :]


def project_out(x, w, after, tiles, n):
    rows, width = x.shape
    rank = w.shape[1]
    out = jax.ShapeDtypeStruct((rank // 2, rows), F32)
    return pl.pallas_call(
        functools.partial(out_kernel, n, tiles),
        in_specs=[in_vmem()] * 2 + [anywhere()],
        out_specs=[in_vmem()] * 2,
        out_shape=[out] * 2,
        scratch_shapes=[pltpu.VMEM((rank, rows), F32)],
        compiler_params=params(16),
        cost_estimate=pl.CostEstimate(
            flops=int(0.5 * 1e9), bytes_accessed=2 * rows * width, transcendentals=0
        ),
        name="project_out",
    )(x, w, after)


def add_kernel(parts, a_ref, b_ref, *rest):
    out_refs = rest[len(rest) - parts :]
    size = a_ref.shape[0] // parts
    for k, out_ref in enumerate(out_refs):
        rows = slice(k * size, (k + 1) * size)
        out_ref[...] = a_ref[rows, :] + b_ref[rows, :]


def add(a, b, parts=1, after=(), weight=0.1):
    out = jax.ShapeDtypeStruct((a.shape[0] // parts, a.shape[1]), F32)
    return pl.pallas_call(
        functools.partial(add_kernel, parts),
        in_specs=[in_vmem()] * 2 + [anywhere()] * len(after),
        out_specs=[in_vmem()] * parts,
        out_shape=[out] * parts,
        compiler_params=params(8),
        cost_estimate=pl.CostEstimate(flops=int(weight * 1e9), bytes_accessed=12 * a.size, transcendentals=0),
        name="add",
    )(a, b, *after)


def add_beside_kernel(a_ref, b_ref, other_ref, sum_ref, same_ref):
    sum_ref[...] = a_ref[...] + b_ref[...]
    same_ref[...] = other_ref[...]


def add_beside(a, b, other, weight):
    return pl.pallas_call(
        add_beside_kernel,
        in_specs=[in_vmem()] * 3,
        out_specs=[in_vmem()] * 2,
        out_shape=[jax.ShapeDtypeStruct(a.shape, F32), jax.ShapeDtypeStruct(other.shape, F32)],
        compiler_params=params(8),
        cost_estimate=pl.CostEstimate(flops=int(weight * 1e9), bytes_accessed=12 * a.size, transcendentals=0),
        name="add_beside",
    )(a, b, other)


def outer_kernel(tokens, group, part, *refs):
    in_refs, (out_ref, grad_ref) = refs[:4], (refs[4], refs[-1])
    width = group * tokens
    rows, rank = in_refs[0].shape
    features = grad_ref.shape[0]
    mine = gray(lax.axis_index("feat")) & 1
    query = lax.broadcasted_iota(jnp.int32, (group, width), 0)
    token = lax.broadcasted_iota(jnp.int32, (group, width), 1)
    own = jnp.where(token // tokens == query, 1.0, 0.0).astype(F32)
    for k, in_ref in enumerate(in_refs):
        half = mine ^ (k // 2)
        for g in range(rows // width):
            step = half * (2 * rows // width) + (k % 2) * (rows // width) + g
            lines = slice(part * features, (part + 1) * features)
            columns = out_ref[lines, pl.ds(pl.multiple_of(step * width, width), width)]
            spread = (columns[:, None, :] * own[None, :, :]).reshape(features * group, width)
            left, left_low = split(spread)
            right, right_low = split(in_ref[g * width : (g + 1) * width, :])
            total = jnp.dot(left, right, preferred_element_type=F32)
            total += jnp.dot(left_low, right, preferred_element_type=F32)
            total += jnp.dot(left, right_low, preferred_element_type=F32)
            place = pl.ds(pl.multiple_of(step * group, group), group)
            grad_ref[:, place, :] = total.reshape(features, group, rank)


def outer(in_pieces, out_columns, tokens, group, part, parts, after=()):
    rank = in_pieces[0].shape[1]
    features, rows = out_columns.shape[0] // parts, out_columns.shape[1]
    out = jax.ShapeDtypeStruct((features, rows // tokens, rank), F32)
    return pl.pallas_call(
        functools.partial(outer_kernel, tokens, group, part),
        in_specs=[in_vmem()] * (len(in_pieces) + 1) + [anywhere()] * len(after),
        out_specs=in_vmem(),
        out_shape=out,
        compiler_params=params(16),
        cost_estimate=pl.CostEstimate(
            flops=6 * rows * group * features * rank, bytes_accessed=8 * rows * rank, transcendentals=0
        ),
        name="outer",
    )(*in_pieces, out_columns, *after)


def split_kernel(first, tiles, x_ref, after_ref, high_ref, low_ref, x_buf, sems):
    del after_ref
    size = x_buf.shape[0] // tiles
    copies = []
    for t in range(tiles):
        copies.append(
            pltpu.make_async_copy(x_ref.at[pl.ds(first + t * size, size)], x_buf.at[pl.ds(t * size, size)], sems.at[t])
        )
        copies[t].start()
    for t in range(tiles):
        copies[t].wait()
        rows = slice(t * size, (t + 1) * size)
        high_ref[rows, :], low_ref[rows, :] = split(x_buf[rows, :])


def split_store(store, after, start, rows):
    width = store.shape[1]
    tiles = tile_count(rows, 16, 5)
    out = jax.ShapeDtypeStruct((rows, width), BF16)
    return pl.pallas_call(
        functools.partial(split_kernel, start, tiles),
        in_specs=[in_hbm(), anywhere()],
        out_specs=[in_vmem()] * 2,
        out_shape=[out] * 2,
        scratch_shapes=[pltpu.VMEM((rows, width), F32), pltpu.SemaphoreType.DMA((tiles,))],
        compiler_params=params(24),
        cost_estimate=pl.CostEstimate(flops=1000 * rows * width, bytes_accessed=0, transcendentals=0),
        name="split_store",
    )(store, after)


def products(grad_refs, store_refs, both, part):
    features, queries, rank = grad_refs[0].shape
    total = len(grad_refs) * queries
    for d, ref in enumerate(grad_refs):
        place = d * queries
        for i in range(features):
            high, low = split(ref[i])
            both[place : place + queries, i * rank : (i + 1) * rank] = high
            both[total + place : total + place + queries, i * rank : (i + 1) * rank] = low
    columns = slice(part * features * rank, (part + 1) * features * rank)
    first = 0
    for high_ref, low_ref in zip(store_refs[::2], store_refs[1::2]):
        sums = lax.dot_general(both[...], high_ref[:, columns], NT, preferred_element_type=F32)
        lows = lax.dot_general(both[:total, :], low_ref[:, columns], NT, preferred_element_type=F32)
        yield slice(first, first + high_ref.shape[0]), sums[:total] + sums[total:] + lows
        first += high_ref.shape[0]


def early_kernel(count, part, *refs):
    store_refs, (result_ref, both) = refs[count:-2], refs[-2:]
    for place, value in products(refs[:count], store_refs, both, part):
        result_ref[:, place] = value


def score_kernel(n, sub, count, part, *refs):
    early_refs, refs = refs[:part], refs[part:]
    store_refs, out_refs, (both, result) = refs[count : -n - 2], refs[-n - 2 : -2], refs[-2:]
    queries = refs[0].shape[1]
    for place, value in products(refs[:count], store_refs, both, part):
        for early_ref in early_refs:
            value = value + early_ref[:, place]
        result[:, place] = value
    own = lax.axis_index("feat") ^ (lax.axis_index("rows") * sub + lax.axis_index("sub"))
    for slot in range(n):
        out_refs[slot][...] = result[pl.ds(pl.multiple_of((own ^ slot) * queries, queries), queries), :]


def score(grads, stored, n, sub, part, parts, early):
    features, queries, rank = grads[0].shape
    examples, width = sum(block.shape[0] for block in stored[::2]), features * rank
    total = len(grads) * queries
    last = part == parts - 1
    if last:
        kernel = functools.partial(score_kernel, n, sub, len(grads), part)
        outs = [jax.ShapeDtypeStruct((total // n, examples), F32)] * n
        scratch = [pltpu.VMEM((total, examples), F32)]
    else:
        kernel = functools.partial(early_kernel, len(grads), part)
        outs, scratch = [jax.ShapeDtypeStruct((total, examples), F32)], []
        early = []
    return pl.pallas_call(
        kernel,
        in_specs=[in_vmem()] * (len(early) + len(grads) + len(stored)),
        out_specs=[in_vmem()] * len(outs),
        out_shape=outs,
        scratch_shapes=[pltpu.VMEM((2 * total, width), BF16), *scratch],
        compiler_params=params(24),
        cost_estimate=pl.CostEstimate(
            flops=6 * total * examples * width, bytes_accessed=4 * examples * width, transcendentals=0
        ),
        name="score",
    )(*early, *grads, *stored)


def tile_count(extent, unit, most):
    return next(t for t in range(most, 0, -1) if extent % (t * unit) == 0)


def local(sizes, acts, out_grads, proj_in, proj_out, store):
    n, rows, sub = sizes["feat"], sizes["rows"], sizes["sub"]
    bits = n.bit_length() - 1
    queries, tokens, width = acts.shape
    flat = queries * tokens
    acts = acts.reshape(flat, width)
    out_grads = out_grads.reshape(flat, width)

    in_send = project_sent(acts, proj_in)
    in_recv = exchange(in_send, "feat", n, 1)
    in_send, *in_keep = project_rest(acts, proj_in, in_send)
    out_keep, out_send = project_out(out_grads, proj_out, in_send, 4, n)
    piece, out_send = add_beside(in_keep[0], in_recv, out_send, 2)
    pieces = [piece, *add(in_keep[1], exchange(in_send, "feat", n, 1), 1, (piece,), 1)]
    examples = store.shape[0]
    early = examples // 512 * 256
    stored = split_store(store, pieces[1], 0, early) if early else []
    for s in range(1, bits):
        mask = 2 ** (s + 1) - 1
        in_recvs = [exchange(piece, "feat", n, mask) for piece in pieces]
        out_keep, out_send = add(out_keep, exchange(out_send, "feat", n, mask // 2), 2, stored[:1])
        out_recv = exchange(out_send, "feat", n, mask)
        (first,) = add(pieces[0], in_recvs[0], 1, (), 1)
        pieces = [first, *add(pieces[1], in_recvs[1], 1, (first,), 1)]
    stored = stored + split_store(store, pieces[1], early, examples - early)
    (out_sum,) = add(out_keep, out_recv, 1, stored[-1:], weight=20)
    others = [exchange(piece, "feat", n, 1) for piece in pieces]

    blocks = [(0, [*pieces, *others], out_sum)]
    mask = 1
    while mask < rows:
        for d, block, out in list(blocks):
            parts = [exchange(part, "rows", rows, mask) for part in (*block, out)]
            blocks.append((d ^ (mask * sub), parts[:-1], parts[-1]))
        mask *= 2
    parts = 2 if out_sum.shape[0] % 16 == 0 else 1
    grads = [{} for _ in range(parts)]
    after = ()
    for d, block, out in blocks:
        for part in range(parts):
            grads[part][d] = outer(block, out, tokens, 8, part, parts, after)
        after = (grads[-1][d],)
    early = []
    for part in range(parts):
        mask = 1
        while mask < sub:
            for d, grad in list(grads[part].items()):
                grads[part][d ^ mask] = exchange(grad, "sub", sub, mask)
            mask *= 2
        ordered = [grads[part][d] for d in range(len(grads[part]))]
        scores = score(ordered, stored, n, sub, part, parts, early)
        early = early + list(scores)
    total = scores[0]
    for mask in sorted(range(1, n), key=lambda m: -(m & -m)):
        (total,) = add(total, exchange(scores[mask], "feat", n, mask), 1, (), 1)
    return total


def solution(mesh):
    return jax.shard_map(
        functools.partial(local, dict(mesh.shape)),
        mesh=mesh,
        in_specs=(
            P(("groups", "rows", "sub"), None, "feat"),
            P(("groups", "rows", "sub"), None, "feat"),
            P("feat", None),
            P("feat", None),
            P(("groups", "rows", "sub"), "feat"),
        ),
        out_specs=P(("groups", "feat"), ("rows", "sub")),
        check_vma=False,
    )
```
